32 devices in a mesh: uly: 4 (over y, x), blk: 8 (over z, core).
Axes of the slice: x: 2, y: 2, z: 4, core: 2. Of those that a mesh axis runs over, the one named last changes fastest.
Arguments:
- query_rows: bfloat16 [12288, 512], P(('uly', 'blk')), may hold values from -8 to 8
- key_rows: bfloat16 [12288, 512], P(('uly', 'blk')), may hold values from -8 to 8
- value_rows: bfloat16 [12288, 512], P(('uly', 'blk')), may hold values from -6 to 6
- kept_tiles: int32 [32, 6], replicated, may hold values from -1 to 31, as said below
Outputs:
- attended: bfloat16 [12288, 512], P(('uly', 'blk'))
The draws below stay inside these ranges and needn't reach their ends.
Inputs may be any that keep to these rules, and one draw needn't show every extreme that they name: `kept_tiles`: tile t = p * 8 + a with p = b * 4 + c has coordinates (b, a, c) with 0 <= b < 1, 0 <= a < 8, 0 <= c < 4; slab a is the tiles with that a, and p is a tile's position in its slab. Row t lists distinct tiles, t itself first, then the others, then -1 in the unused entries; every listed tile differs from t by at most 1 in each coordinate. For every slab a and each of the slabs a - 1 and a + 1, the tiles of that neighbouring slab listed by queries of slab a lie within 2 consecutive positions. Some row fills all 6 entries.
All inputs are finite; a program needn't handle non-finite values.
Results may differ from the reference program's by a relative error of at most 0.0047.
Values may be sent and summed in bfloat16 or wider, within the bound.
A program may use at most 64 MiB of HBM per device.

```python
import jax
import jax.numpy as jnp
from jax import lax

HEAD_DIM = 128
TILE = 384
KEEP = 6
TC = 4
HEADS = 4
TA = 8
TB = 1
SLAB = 4
USED = 2
TILES = 32
TOKENS = 12288


def normal_base(key):
    return jnp.clip(jax.random.normal(key, (TOKENS, HEADS * HEAD_DIM), jnp.float32), -6.0, 6.0)


def draw_query_rows(key, part):
    result = normal_base(jax.random.fold_in(key, 5))
    return result.astype(jnp.bfloat16)


def draw_key_rows(key, part):
    result = normal_base(jax.random.fold_in(key, 6))
    return result.astype(jnp.bfloat16)


def draw_kept_tiles(key, part):
    run_starts = jax.random.randint(jax.random.fold_in(key, 11), (TA, 2), 0, SLAB - USED + 1)
    tile_ids = jnp.arange(TILES, dtype=jnp.int32)
    coord_a = tile_ids % TA
    slab_pos = tile_ids // TA
    coord_b = slab_pos // TC
    coord_c = slab_pos % TC
    offset_ids = jnp.arange(27, dtype=jnp.int32)
    shift_b = offset_ids // 9 - 1
    shift_a = offset_ids // 3 % 3 - 1
    shift_c = offset_ids % 3 - 1
    key_b = coord_b[:, None] + shift_b[None, :]
    key_a = coord_a[:, None] + shift_a[None, :]
    key_c = coord_c[:, None] + shift_c[None, :]
    inside = (key_b >= 0) & (key_b < TB) & (key_a >= 0) & (key_a < TA) & (key_c >= 0) & (key_c < TC)
    position = key_b * TC + key_c
    side_index = jnp.where(shift_a > 0, 1, 0)
    run_low = run_starts[coord_a[:, None], side_index[None, :]]
    in_run = (position >= run_low) & (position < run_low + USED)
    allowed = inside & ((shift_a == 0)[None, :] | in_run)
    own_offset = (shift_a == 0) & (shift_b == 0) & (shift_c == 0)
    direct = (shift_a != 0) & (shift_b == 0) & (shift_c == 0)
    forced = allowed & direct[None, :]
    level = jnp.where(own_offset[None, :], 3, jnp.where(forced, 2, jnp.where(allowed, 1, 0)))
    noise = jax.random.randint(jax.random.fold_in(key, 12), (TILES, 27), 0, 1 << 20)
    ranking = level * (1 << 26) + noise * 32 + jnp.arange(27, dtype=jnp.int32)[None, :]
    ranked, chosen = lax.top_k(ranking, KEEP)
    count_live = jnp.sum(allowed.astype(jnp.int32), axis=1)
    count_forced = jnp.sum((level >= 2).astype(jnp.int32), axis=1)
    wanted = jax.random.randint(jax.random.fold_in(key, 13), (TILES,), 3, KEEP + 1)
    wanted = jnp.where(tile_ids % 4 == 0, KEEP, wanted)
    chosen_pos = run_starts[1, 1] + USED // 2
    chosen_tile = chosen_pos * TA + 1
    wanted = jnp.where(tile_ids == chosen_tile, KEEP, wanted)
    live_count = jnp.minimum(jnp.maximum(wanted, count_forced), count_live)
    key_tile = (key_b * TC + key_c) * TA + key_a
    picked = jnp.take_along_axis(key_tile, chosen, axis=1)
    slot_index = jnp.arange(KEEP, dtype=jnp.int32)
    return jnp.where(slot_index[None, :] < live_count[:, None], picked, -1).astype(jnp.int32)


def shard_levels(rng, extent, pieces, low, largest):
    loudness, own = 1.0, jax.random.fold_in(rng, 6)
    for axis_at, blocks in pieces:
        heights = jnp.exp(jax.random.uniform(jax.random.fold_in(own, axis_at), (blocks,), jnp.float32, low / len(pieces), largest / len(pieces)))
        loudness = loudness * jnp.repeat(heights, extent[axis_at] // blocks).reshape([-1 if axis == axis_at else 1 for axis in range(len(extent))])
    return loudness


def bell_draw(own_key, shape, scale, bound, pieces=(), held_as=jnp.bfloat16):
    drawn = jax.random.normal(own_key, shape, jnp.float32) * scale
    if len(pieces) > 0:
        drawn = shard_levels(own_key, shape, pieces, -0.22, 0.18) * drawn
    return jnp.clip(drawn, min=-bound, max=bound).astype(held_as)


def setup_inputs(seed: int = 0) -> dict:
    seeds = jax.random.split(jax.random.key(seed), 5)
    query_rows = draw_query_rows(jax.random.fold_in(seeds[4], 71), 0)
    key_rows = draw_key_rows(jax.random.fold_in(seeds[4], 71), 0)
    value_rows = bell_draw(seeds[2], (TOKENS, HEADS * HEAD_DIM), 1.0, 6.0, ((0, 32),))
    kept_tiles = draw_kept_tiles(jax.random.fold_in(seeds[4], 71), 0)
    return dict(query_rows=query_rows, key_rows=key_rows, value_rows=value_rows, kept_tiles=kept_tiles)


def reference(query_rows, key_rows, value_rows, kept_tiles):
    score_scale = HEAD_DIM ** -0.5
    query_tiles = query_rows.reshape(TILES, TILE, HEADS, HEAD_DIM)
    key_tiles = key_rows.reshape(TILES, TILE, HEADS, HEAD_DIM)
    value_tiles = value_rows.reshape(TILES, TILE, HEADS, HEAD_DIM)

    def attend_tile(tile_id):
        listed = kept_tiles[tile_id]
        is_live = listed >= 0
        safe_ids = jnp.where(is_live, listed, 0).astype(jnp.int32)
        key_gather = key_tiles[safe_ids].astype(jnp.float32)
        value_gather = value_tiles[safe_ids].astype(jnp.float32)
        query_block = query_tiles[tile_id].astype(jnp.float32)
        scores = jnp.einsum("ihd,kjhd->hikj", query_block, key_gather) * score_scale
        scores = jnp.where(is_live[None, None, :, None], scores, -jnp.inf)
        row_max = jnp.max(scores, axis=(2, 3), keepdims=True)
        weights = jnp.exp(scores - row_max)
        totals = jnp.sum(weights, axis=(2, 3))
        weights_low = lax.optimization_barrier(weights.astype(jnp.bfloat16)).astype(jnp.float32)
        mixed = jnp.einsum("hikj,kjhd->ihd", weights_low, value_gather)
        mixed = mixed / jnp.transpose(totals)[:, :, None]
        return mixed.astype(jnp.bfloat16)

    attended = lax.map(attend_tile, jnp.arange(TILES, dtype=jnp.int32))
    return attended.reshape(TOKENS, HEADS * HEAD_DIM)
```

```python
import functools
import math

import jax
import jax.numpy as jnp
from jax import lax
from jax.experimental import pallas as pl
from jax.experimental.pallas import tpu as pltpu
from jax.sharding import PartitionSpec as P

HEAD_DIM = 128
TILE = 384
KEEP = 6
MESH = pl.DeviceIdType.MESH
EXP_SCALE = HEAD_DIM ** (-0.5) * math.log2(math.e)


def partner(me, step, n):
    found, bit = me, 1
    while bit < n:
        found = found + ((step // bit) % 2) * bit * (1 - 2 * ((me // bit) % 2))
        bit *= 2
    return found


def kernel(n_uly, n_blk, kept, q_in, k_in, v_in, out, q_buf, k_buf, v_buf, o_buf,
           split_send, split_recv, own_sem, halo_send, halo_recv, out_send, out_recv, out_sem):
    me = lax.axis_index("uly")
    slab = lax.axis_index("blk")
    has_prev, has_next = slab > 0, slab < n_blk - 1
    sides = ((has_prev, slab - 1, 2), (has_next, slab + 1, 0))

    def head_of(ref, head):
        return ref.at[:, pl.ds(pl.multiple_of(head * HEAD_DIM, HEAD_DIM), HEAD_DIM)]

    arrays = ((k_in, k_buf, n_uly), (v_in, v_buf, n_uly), (q_in, q_buf, 0))

    def split(kind, step):
        source, target, base = arrays[kind]
        peer = partner(me, step, n_uly)
        return pltpu.make_async_remote_copy(
            src_ref=head_of(source, peer), dst_ref=target.at[base + me],
            send_sem=split_send.at[kind, step], recv_sem=split_recv.at[kind, step],
            device_id=(peer, slab), device_id_type=MESH)

    def own(kind):
        source, target, base = arrays[kind]
        return pltpu.make_async_copy(head_of(source, me), target.at[base + me], own_sem.at[kind])

    def halo(kind, step, side):
        _, other, slot = sides[side]
        source, target, base = arrays[kind]
        position = partner(me, step, n_uly)
        held = head_of(source, me) if isinstance(step, int) and step == 0 else target.at[base + position]
        return pltpu.make_async_remote_copy(
            src_ref=held, dst_ref=target.at[slot * n_uly + position],
            send_sem=halo_send.at[kind, side, step], recv_sem=halo_recv.at[kind, side, step],
            device_id=(me, other), device_id_type=MESH)

    def give(step):
        peer = partner(me, step, n_uly)
        return pltpu.make_async_remote_copy(
            src_ref=o_buf.at[step], dst_ref=head_of(out, me),
            send_sem=out_send.at[step], recv_sem=out_recv.at[step],
            device_id=(peer, slab), device_id_type=MESH)

    barrier = pltpu.get_barrier_semaphore()
    for step in range(1, n_uly):
        pl.semaphore_signal(barrier, inc=1, device_id=(partner(me, step, n_uly), slab), device_id_type=MESH)
    for there, other, _ in sides:
        @pl.when(there)
        def _():
            pl.semaphore_signal(barrier, inc=1, device_id=(me, other), device_id_type=MESH)
    for kind in range(3):
        own(kind).start()
    pl.semaphore_wait(barrier, n_uly - 1 + has_prev.astype(jnp.int32) + has_next.astype(jnp.int32))

    order = [n_uly - 1] + list(range(1, n_uly - 1))
    for kind in range(2):
        for step in order:
            split(kind, step).start()
    for side, (there, _, _) in enumerate(sides):
        @pl.when(there)
        def _():
            for kind in range(2):
                halo(kind, 0, side).start()
    for step in order:
        split(2, step).start()
    for kind in range(2):
        for step in order:
            split(kind, step).wait_recv()
            for side, (there, _, _) in enumerate(sides):
                @pl.when(there)
                def _():
                    halo(kind, step, side).start()
    for kind in range(3):
        own(kind).wait()
    for side, (there, _, _) in enumerate(sides):
        @pl.when(there)
        def _():
            for kind in range(2):
                for step in range(n_uly):
                    halo(kind, step, 1 - side).wait_recv()

    def attend(turn, carry):
        step = lax.rem(turn + 1, n_uly)
        position = partner(me, step, n_uly)

        @pl.when(step > 0)
        def _():
            split(2, step).wait_recv()

        query = q_buf[position]
        slots, lifts = [], []
        for entry in range(KEEP):
            listed = kept[position * n_blk + slab, entry]
            live = listed >= 0
            slot = (listed % n_blk - slab + 1) * n_uly + listed // n_blk
            slots.append(jnp.clip(jnp.where(live, slot, n_uly + position), 0, 3 * n_uly - 1))
            lifts.append(jnp.where(live, 0.0, jnp.inf).astype(jnp.float32))
        scores, top = [], None
        for slot in slots:
            part = lax.dot_general(query, k_buf[slot], (((1,), (1,)), ((), ())),
                                   preferred_element_type=jnp.float32)
            scores.append(part)
            top = part if top is None else jnp.maximum(top, part)
        row_max = jnp.max(top, axis=1, keepdims=True) * EXP_SCALE
        mixed, sums = None, None
        for slot, lift, part in zip(slots, lifts, scores):
            weights = jnp.exp2(part * EXP_SCALE - (row_max + lift))
            sums = weights if sums is None else sums + weights
            term = jnp.dot(weights.astype(jnp.bfloat16), v_buf[slot], preferred_element_type=jnp.float32)
            mixed = term if mixed is None else mixed + term
        totals = jnp.sum(sums, axis=1, keepdims=True)
        o_buf[step] = (mixed / totals).astype(jnp.bfloat16)

        @pl.when(step > 0)
        def _():
            give(step).start()

        return carry

    lax.fori_loop(0, n_uly, attend, 0)
    last = pltpu.make_async_copy(o_buf.at[0], head_of(out, me), out_sem)
    last.start()
    for kind in range(3):
        for step in order:
            split(kind, step).wait_send()
    for side, (there, _, _) in enumerate(sides):
        @pl.when(there)
        def _():
            for kind in range(2):
                for step in range(n_uly):
                    halo(kind, step, side).wait_send()
    for step in order:
        peer = partner(me, step, n_uly)
        give(step).wait_send()
        pltpu.make_async_remote_copy(
            src_ref=o_buf.at[step], dst_ref=head_of(out, peer),
            send_sem=out_send.at[step], recv_sem=out_recv.at[step],
            device_id=(peer, slab), device_id_type=MESH).wait_recv()
    last.wait()


def body(n_uly, n_blk, query_rows, key_rows, value_rows, kept_tiles):
    flops = 4 * n_uly * KEEP * TILE * TILE * HEAD_DIM
    dma = pltpu.SemaphoreType.DMA
    tile = (TILE, HEAD_DIM)
    return pl.pallas_call(
        functools.partial(kernel, n_uly, n_blk),
        out_shape=jax.ShapeDtypeStruct(query_rows.shape, query_rows.dtype),
        in_specs=[pl.BlockSpec(memory_space=pltpu.SMEM)] + [pl.BlockSpec(memory_space=pl.ANY)] * 3,
        out_specs=pl.BlockSpec(memory_space=pltpu.VMEM),
        scratch_shapes=[
            pltpu.VMEM((n_uly, *tile), jnp.bfloat16),
            pltpu.VMEM((3 * n_uly, *tile), jnp.bfloat16),
            pltpu.VMEM((3 * n_uly, *tile), jnp.bfloat16),
            pltpu.VMEM((n_uly, *tile), jnp.bfloat16),
            dma((3, n_uly)), dma((3, n_uly)), dma((3,)),
            dma((2, 2, n_uly)), dma((2, 2, n_uly)),
            dma((n_uly,)), dma((n_uly,)), dma,
        ],
        compiler_params=pltpu.CompilerParams(
            collective_id=0, has_side_effects=True, vmem_limit_bytes=48 * 2**20),
        cost_estimate=pl.CostEstimate(
            flops=flops, bytes_accessed=8 * TILE * n_uly * HEAD_DIM,
            transcendentals=n_uly * KEEP * TILE * TILE),
    )(kept_tiles, query_rows, key_rows, value_rows)


def solution(mesh):
    rows = P(("uly", "blk"), None)
    return jax.shard_map(
        functools.partial(body, mesh.shape["uly"], mesh.shape["blk"]),
        mesh=mesh, in_specs=(rows, rows, rows, P()), out_specs=rows, check_vma=False)
```

```python
import functools
import math

import jax
import jax.numpy as jnp
from jax import lax
from jax.experimental import pallas as pl
from jax.experimental.pallas import tpu as pltpu
from jax.sharding import PartitionSpec as P

HEAD_DIM = 128
TILE = 384
KEEP = 6
MESH = pl.DeviceIdType.MESH
EXP_SCALE = HEAD_DIM ** (-0.5) * math.log2(math.e)


def partner(me, step, n):
    found, bit = me, 1
    while bit < n:
        found = found + ((step // bit) % 2) * bit * (1 - 2 * ((me // bit) % 2))
        bit *= 2
    return found


def kernel(n_uly, n_blk, kept_in, q_in, k_in, v_in, out, q_buf, k_buf, v_buf, o_buf,
           split_send, split_recv, own_sem, halo_send, halo_recv, out_send, out_recv, out_sem, kept, kept_sem):
    me = lax.axis_index("uly")
    slab = lax.axis_index("blk")
    has_prev, has_next = slab > 0, slab < n_blk - 1
    sides = ((has_prev, slab - 1, 2), (has_next, slab + 1, 0))

    def head_of(ref, head):
        return ref.at[:, pl.ds(pl.multiple_of(head * HEAD_DIM, HEAD_DIM), HEAD_DIM)]

    arrays = ((k_in, k_buf, n_uly), (v_in, v_buf, n_uly), (q_in, q_buf, 0))

    def split(kind, step):
        source, target, base = arrays[kind]
        peer = partner(me, step, n_uly)
        return pltpu.make_async_remote_copy(
            src_ref=head_of(source, peer), dst_ref=target.at[base + me],
            send_sem=split_send.at[kind, step], recv_sem=split_recv.at[kind, step],
            device_id=(peer, slab), device_id_type=MESH)

    def own(kind):
        source, target, base = arrays[kind]
        return pltpu.make_async_copy(head_of(source, me), target.at[base + me], own_sem.at[kind])

    def halo(kind, step, side):
        _, other, slot = sides[side]
        source, target, base = arrays[kind]
        position = partner(me, step, n_uly)
        held = head_of(source, me) if isinstance(step, int) and step == 0 else target.at[base + position]
        return pltpu.make_async_remote_copy(
            src_ref=held, dst_ref=target.at[slot * n_uly + position],
            send_sem=halo_send.at[kind, side, step], recv_sem=halo_recv.at[kind, side, step],
            device_id=(me, other), device_id_type=MESH)

    def give(step):
        peer = partner(me, step, n_uly)
        return pltpu.make_async_remote_copy(
            src_ref=o_buf.at[step], dst_ref=head_of(out, me),
            send_sem=out_send.at[step], recv_sem=out_recv.at[step],
            device_id=(peer, slab), device_id_type=MESH)

    barrier = pltpu.get_barrier_semaphore()
    for step in range(1, n_uly):
        pl.semaphore_signal(barrier, inc=1, device_id=(partner(me, step, n_uly), slab), device_id_type=MESH)
    for there, other, _ in sides:
        @pl.when(there)
        def _():
            pl.semaphore_signal(barrier, inc=1, device_id=(me, other), device_id_type=MESH)
    for kind in range(3):
        own(kind).start()
    lists = pltpu.make_async_copy(kept_in, kept, kept_sem)
    lists.start()
    pl.semaphore_wait(barrier, n_uly - 1 + has_prev.astype(jnp.int32) + has_next.astype(jnp.int32))

    order = [n_uly - 1] + list(range(1, n_uly - 1))
    for kind in range(2):
        for step in order:
            split(kind, step).start()
    for side, (there, _, _) in enumerate(sides):
        @pl.when(there)
        def _():
            for kind in range(2):
                halo(kind, 0, side).start()
    for step in order:
        split(2, step).start()
    for kind in range(2):
        for step in order:
            split(kind, step).wait_recv()
            for side, (there, _, _) in enumerate(sides):
                @pl.when(there)
                def _():
                    halo(kind, step, side).start()
    for kind in range(3):
        own(kind).wait()
    lists.wait()
    for side, (there, _, _) in enumerate(sides):
        @pl.when(there)
        def _():
            for kind in range(2):
                for step in range(n_uly):
                    halo(kind, step, 1 - side).wait_recv()

    def attend(turn, carry):
        step = jnp.where(turn == 0, n_uly - 1, jnp.where(turn == n_uly - 1, 0, turn))
        position = partner(me, step, n_uly)

        @pl.when(step > 0)
        def _():
            split(2, step).wait_recv()

        query = q_buf[position]
        slots, lifts = [], []
        for entry in range(KEEP):
            listed = kept[position * n_blk + slab, entry]
            live = listed >= 0
            slot = (listed % n_blk - slab + 1) * n_uly + listed // n_blk
            slots.append(jnp.clip(jnp.where(live, slot, n_uly + position), 0, 3 * n_uly - 1))
            lifts.append(jnp.where(live, 0.0, jnp.inf).astype(jnp.float32))
        scores, top = [], None
        for slot in slots:
            part = lax.dot_general(query, k_buf[slot], (((1,), (1,)), ((), ())),
                                   preferred_element_type=jnp.float32)
            scores.append(part)
            top = part if top is None else jnp.maximum(top, part)
        row_max = jnp.max(top, axis=1, keepdims=True) * EXP_SCALE
        mixed, sums = None, None
        for slot, lift, part in zip(slots, lifts, scores):
            weights = jnp.exp2(part * EXP_SCALE - (row_max + lift))
            sums = weights if sums is None else sums + weights
            term = jnp.dot(weights.astype(jnp.bfloat16), v_buf[slot], preferred_element_type=jnp.float32)
            mixed = term if mixed is None else mixed + term
        totals = jnp.sum(sums, axis=1, keepdims=True)
        o_buf[step] = (mixed / totals).astype(jnp.bfloat16)

        @pl.when(step > 0)
        def _():
            give(step).start()

        return carry

    lax.fori_loop(0, n_uly, attend, 0)
    last = pltpu.make_async_copy(o_buf.at[0], head_of(out, me), out_sem)
    last.start()
    for kind in range(3):
        for step in order:
            split(kind, step).wait_send()
    for side, (there, _, _) in enumerate(sides):
        @pl.when(there)
        def _():
            for kind in range(2):
                for step in range(n_uly):
                    halo(kind, step, side).wait_send()
    for step in order:
        peer = partner(me, step, n_uly)
        give(step).wait_send()
        pltpu.make_async_remote_copy(
            src_ref=o_buf.at[step], dst_ref=head_of(out, peer),
            send_sem=out_send.at[step], recv_sem=out_recv.at[step],
            device_id=(peer, slab), device_id_type=MESH).wait_recv()
    last.wait()


def body(n_uly, n_blk, query_rows, key_rows, value_rows, kept_tiles):
    flops = 4 * n_uly * KEEP * TILE * TILE * HEAD_DIM
    dma = pltpu.SemaphoreType.DMA
    tile = (TILE, HEAD_DIM)
    return pl.pallas_call(
        functools.partial(kernel, n_uly, n_blk),
        out_shape=jax.ShapeDtypeStruct(query_rows.shape, query_rows.dtype),
        in_specs=[pl.BlockSpec(memory_space=pltpu.HBM)] * 4,
        out_specs=pl.BlockSpec(memory_space=pltpu.VMEM),
        scratch_shapes=[
            pltpu.VMEM((n_uly, *tile), jnp.bfloat16),
            pltpu.VMEM((3 * n_uly, *tile), jnp.bfloat16),
            pltpu.VMEM((3 * n_uly, *tile), jnp.bfloat16),
            pltpu.VMEM((n_uly, *tile), jnp.bfloat16),
            dma((3, n_uly)), dma((3, n_uly)), dma((3,)),
            dma((2, 2, n_uly)), dma((2, 2, n_uly)),
            dma((n_uly,)), dma((n_uly,)), dma,
            pltpu.SMEM(kept_tiles.shape, jnp.int32), dma,
        ],
        compiler_params=pltpu.CompilerParams(
            collective_id=0, has_side_effects=True, vmem_limit_bytes=48 * 2**20),
        cost_estimate=pl.CostEstimate(
            flops=flops, bytes_accessed=8 * TILE * n_uly * HEAD_DIM,
            transcendentals=n_uly * KEEP * TILE * TILE),
    )(kept_tiles, query_rows, key_rows, value_rows)


def solution(mesh):
    rows = P(("uly", "blk"), None)
    return jax.shard_map(
        functools.partial(body, mesh.shape["uly"], mesh.shape["blk"]),
        mesh=mesh, in_specs=(rows, rows, rows, P()), out_specs=rows, check_vma=False)
```
